32 devices in a mesh: exp: 8 (over y, x, core), attn: 4 (over z).
Axes of the slice: x: 2, y: 2, z: 4, core: 2. Of those that a mesh axis runs over, the one named last changes fastest.
Arguments:
- tokens: bfloat16 [1024, 2048], P('exp', 'attn'), may hold values from -6 to 6
- cotangent: bfloat16 [1024, 2048], P('exp', 'attn'), may hold values from -6 to 6
- expert_ids: int32 [1024, 2], P('exp'), may hold values from 0 to 7, all different within a row; in each aligned block of 128 rows (0 to 127, 128 to 255, ...) at most 48 rows name the same one
- route_weight: bfloat16 [1024, 2], P('exp'), may hold values from 0.099609375 to 1
- gate_weight: bfloat16 [8, 2048, 768], P('exp', 'attn'), may hold values from -0.125 to 0.125
- up_weight: bfloat16 [8, 2048, 768], P('exp', 'attn'), may hold values from -0.125 to 0.125
- down_weight: bfloat16 [8, 768, 2048], P('exp', None, 'attn'), may hold values from -0.21875 to 0.21875
Outputs:
- grad_tokens: bfloat16 [1024, 2048], P('exp', 'attn')
- grad_route: float32 [1024, 2], P('exp')
- grad_gate: float32 [8, 2048, 768], P('exp', 'attn')
- grad_up: float32 [8, 2048, 768], P('exp', 'attn')
- grad_down: float32 [8, 768, 2048], P('exp', None, 'attn')
The draws below stay inside these ranges and needn't reach their ends.
Inputs may be any that keep to these rules, and one draw needn't show every extreme that they name: `expert_ids`: each row names 2 different experts. Within the 128 tokens of one index of exp (aligned blocks of rows), no expert is named by more than 48 choices, and in every draw some block names some expert exactly 48 times.
All inputs are finite; a program needn't handle non-finite values.
Results may differ from the reference program's by a relative error of at most 0.028.
Values may be sent and summed in bfloat16 or wider, within the bound.
A program may use at most 64 MiB of HBM per device.

```python
import math
import jax
import jax.numpy as jnp
import numpy as np
from jax import lax

D = 2048
H = 768
TOK_DEV = 128
TOPW = 2
EXPERTS = 8
CAP = 48
ROWS = 384
TOKENS = 1024
N_EXP = 8
N_ATTN = 4


def shard_levels(key, shape, split, least, largest):
    gain, own = 1.0, jax.random.fold_in(key, 6)
    for position, shards_of in split:
        steps = jnp.exp(jax.random.uniform(jax.random.fold_in(own, position), (shards_of,), jnp.float32, least / len(split), largest / len(split)))
        gain = gain * jnp.repeat(steps, shape[position] // shards_of).reshape([-1 if axis == position else 1 for axis in range(len(shape))])
    return gain


def deal_out(own_key, own, number, rows, amount, top, most, slope):
    sequence = jax.random.permutation(own_key, amount)
    packed, common = load_shares(amount, rows * top, most, slope, True), load_shares(amount, rows * top, most, slope, False)
    places = jnp.arange(amount)

    def named(sizes, rotation):
        used = int((sizes > 0).sum())
        fixed = max(1, used // 4)
        passed = fixed + (places - fixed + rotation * (used - fixed)) % max(1, amount - fixed)
        return jnp.zeros((amount,), jnp.int32).at[sequence[jnp.where(places < fixed, places, passed)]].set(jnp.asarray(sizes, jnp.int32))

    sizes = jnp.where(number % 4 == 0, named(packed, number // 4), named(common, number - number // 4 - 1))
    mixed = jax.random.permutation(jax.random.fold_in(own, 3), amount)
    giver, receiver = mixed[0:amount // 2 * 2:2], mixed[1:amount // 2 * 2:2]
    room = jnp.minimum(sizes[giver] - 1, most - sizes[receiver]) // 2
    room = jnp.where((giver == sequence[0]) | (receiver == sequence[0]) | (sizes[receiver] == 0), 0, jnp.maximum(room, 0))
    passed = jax.random.randint(jax.random.fold_in(own, 4), (amount // 2,), 0, 1 << 20) % (room + 1)
    sizes = sizes.at[giver].add(-passed).at[receiver].add(passed)
    labels = jnp.searchsorted(jnp.cumsum(sizes), jnp.arange(rows * top), side="right").astype(jnp.int32)
    grid = labels.reshape(top, rows).T
    grid = grid[jax.random.permutation(jax.random.fold_in(own, 1), rows)]
    rotation = jax.random.randint(jax.random.fold_in(own, 2), (rows, 1), 0, top)
    return jnp.take_along_axis(grid, (jnp.arange(top)[None, :] + rotation) % top, axis=1)


def load_shares(amount, total, most, skew, full):
    portions = [(1 << 20) // math.isqrt(grade ** skew) + 1 for grade in range(1, amount + 1)]
    largest = most if full else min(most, max(-(-total // amount), total * portions[0] // sum(portions)))
    least = 1 if total - largest >= amount - 1 else 0
    counts, surplus = [largest] + [least] * (amount - 1), total - largest - least * (amount - 1)
    while surplus > 0:
        free = [i for i in range(1, amount) if counts[i] < largest] or [i for i in range(1, amount) if counts[i] < most]
        mass, budget = sum([portions[i] for i in free]), surplus
        for i in free:
            extra = min(most - counts[i], max(1, budget * portions[i] // mass), surplus)
            counts[i] = counts[i] + extra
            surplus = surplus - extra
    return np.array(counts)


def noise(key, dims, scale, most, shards=(), kind=jnp.bfloat16):
    level = shard_levels(key, dims, shards, -0.22, 0.18) if shards else 1.0
    values = jax.random.normal(key, dims, jnp.float32) * scale * level
    return jnp.minimum(jnp.maximum(values, -most), most).astype(kind)


def setup_inputs(seed: int = 0) -> dict:
    key_of = jax.random.split(jax.random.key(seed), 8)
    tokens = noise(key_of[0], (TOKENS, D), 1.0, 6.0, ((0, 8), (1, 4)))
    cotangent = noise(key_of[1], (TOKENS, D), 1.0, 6.0, ((0, 8), (1, 4)))
    expert_ids_keys = jax.random.split(jax.random.fold_in(key_of[2], 1), TOKENS // TOK_DEV)
    expert_ids_turns = jax.random.permutation(jax.random.fold_in(key_of[2], 3), TOKENS // TOK_DEV)
    expert_ids = jax.vmap(lambda own, number: deal_out(jax.random.fold_in(key_of[2], 2), own, number, TOK_DEV, EXPERTS, TOPW, CAP, 2))(expert_ids_keys, expert_ids_turns).reshape((TOKENS, TOPW))
    route_weight = jnp.clip(jnp.exp(math.log(1.0) - 2.306499 * jax.random.uniform(key_of[3], (TOKENS, TOPW), jnp.float32) ** shard_levels(key_of[3], (TOKENS, TOPW), ((0, 8),), -0.2, 0.2)), 0.099609375, 1.0).astype(jnp.bfloat16)
    gate_weight = noise(key_of[4], (EXPERTS, D, H), D ** -0.5, 0.125, ((0, 8), (1, 4)))
    up_weight = noise(key_of[5], (EXPERTS, D, H), D ** -0.5, 0.125, ((0, 8), (1, 4)))
    down_weight = noise(key_of[6], (EXPERTS, H, D), H ** -0.5, 0.21875, ((0, 8), (2, 4)))
    return dict(tokens=tokens, cotangent=cotangent, expert_ids=expert_ids, route_weight=route_weight, gate_weight=gate_weight, up_weight=up_weight, down_weight=down_weight)


def slice_sums(left_side, right_side):
    row_total = left_side.shape[0]
    partials = jnp.einsum('rnd,ndh->nrh', left_side.reshape(row_total, N_ATTN, -1).astype(jnp.float32), right_side.reshape(N_ATTN, -1, right_side.shape[1]).astype(jnp.float32))
    rounded = lax.optimization_barrier(partials.astype(jnp.bfloat16))
    return jnp.sum(rounded.astype(jnp.float32), axis=0)


def reference(tokens, cotangent, expert_ids, route_weight, gate_weight, up_weight, down_weight):
    per_block = TOK_DEV * TOPW
    routed = expert_ids.reshape(N_EXP, per_block)
    one_hot = (routed[:, :, None] == jnp.arange(EXPERTS, dtype=jnp.int32)[None, None, :]).astype(jnp.int32)
    ranked = jnp.cumsum(one_hot, axis=1) - 1
    slot_pos = jnp.sum(ranked * one_hot, axis=2)
    sources = jnp.arange(N_EXP, dtype=jnp.int32)[:, None]
    column = (sources * CAP + slot_pos).astype(jnp.int32)
    row_index = (sources * per_block + jnp.arange(per_block, dtype=jnp.int32)[None, :]).astype(jnp.int32)
    slot_table = jnp.full((EXPERTS, ROWS), N_EXP * per_block, jnp.int32).at[routed, column].set(row_index)
    feat_all = jnp.concatenate([jnp.repeat(tokens, TOPW, axis=0), jnp.zeros((1, D), jnp.bfloat16)], axis=0)
    upstream_all = jnp.concatenate([jnp.repeat(cotangent, TOPW, axis=0), jnp.zeros((1, D), jnp.bfloat16)], axis=0)
    weight_all = jnp.concatenate([route_weight.reshape(-1), jnp.zeros((1,), jnp.bfloat16)], axis=0)

    def one_expert(inputs):
        table_row, gate_w, up_w, down_w = inputs
        feat_rows = feat_all[table_row]
        upstream_rows = upstream_all[table_row]
        weight_rows = weight_all[table_row]
        scaled_rows = (weight_rows[:, None].astype(jnp.float32) * upstream_rows.astype(jnp.float32)).astype(jnp.bfloat16)
        gate_sum = slice_sums(feat_rows, gate_w)
        up_sum = slice_sums(feat_rows, up_w)
        back_sum = slice_sums(scaled_rows, down_w.T)
        sigmoid_gate = jax.nn.sigmoid(gate_sum)
        silu_gate = gate_sum * sigmoid_gate
        activation = (silu_gate * up_sum).astype(jnp.bfloat16)
        grad_g = (back_sum * up_sum * sigmoid_gate * (1.0 + gate_sum * (1.0 - sigmoid_gate))).astype(jnp.bfloat16)
        grad_u = (back_sum * silu_gate).astype(jnp.bfloat16)
        grad_gate_e = jnp.dot(feat_rows.T, grad_g, preferred_element_type=jnp.float32)
        grad_up_e = jnp.dot(feat_rows.T, grad_u, preferred_element_type=jnp.float32)
        grad_down_e = jnp.dot(activation.T, scaled_rows, preferred_element_type=jnp.float32)
        term_rows = (jnp.dot(grad_g, gate_w.T, preferred_element_type=jnp.float32) + jnp.dot(grad_u, up_w.T, preferred_element_type=jnp.float32)).astype(jnp.bfloat16)
        out_rows = jnp.dot(activation, down_w, preferred_element_type=jnp.float32)
        score_parts = jnp.sum((upstream_rows.astype(jnp.float32) * out_rows).reshape(ROWS, N_ATTN, -1), axis=2)
        score_rounded = lax.optimization_barrier(score_parts.astype(jnp.bfloat16))
        score_rows = jnp.sum(score_rounded.astype(jnp.float32), axis=1)
        return grad_gate_e, grad_up_e, grad_down_e, term_rows, score_rows

    grad_gate, grad_up, grad_down, term_all, score_all = lax.map(one_expert, (slot_table, gate_weight, up_weight, down_weight))
    flat_table = slot_table.reshape(-1)
    token_sums = jnp.zeros((N_EXP * per_block + 1, D), jnp.float32).at[flat_table].add(term_all.reshape(-1, D).astype(jnp.float32))
    grad_tokens = jnp.sum(token_sums[:-1].reshape(TOKENS, TOPW, D), axis=1).astype(jnp.bfloat16)
    score_sums = jnp.zeros((N_EXP * per_block + 1,), jnp.float32).at[flat_table].add(score_all.reshape(-1))
    grad_route = score_sums[:-1].reshape(TOKENS, TOPW)
    return grad_tokens, grad_route, grad_gate, grad_up, grad_down
```

```python
import functools

import jax
import jax.numpy as jnp
from jax import lax
from jax.experimental import pallas as pl
from jax.experimental.pallas import tpu as pltpu
from jax.sharding import PartitionSpec as P

MESH = pl.DeviceIdType.MESH
F32 = jnp.float32
BF16 = jnp.bfloat16
LAG = 3


def partner_of(me, step, count):
    total, bit = 0, 1
    while bit < count:
        total = total + lax.rem(lax.div(me, bit) + lax.div(step, bit), 2) * bit
        bit *= 2
    return total


def contract_rows(left, right):
    return lax.dot_general(left, right, (((0,), (0,)), ((), ())), preferred_element_type=F32)


def contract_columns(left, right):
    return lax.dot_general(left, right, (((1,), (1,)), ((), ())), preferred_element_type=F32)


def block_kernel(
    experts, attn, cap,
    tok_ref, cot_ref, ids_ref, wt_ref, gate_ref, up_ref, down_ref,
    gtok_ref, route_ref, ggate_ref, gup_ref, gdown_ref,
    x_send, z_send, x_all, z_all, own, from_left, from_right, to_left, to_right, sums,
    act_all, gg_all, gu_all, term_send, term_back, acc_gate, acc_up, acc_down,
    place, score_send, score_back,
    x_ss, x_rs, z_ss, z_rs, r_ss, r_rs, l_ss, l_rs, t_ss, t_rs, s_ss, s_rs, out_sem,
):
    me = lax.axis_index("exp")
    za = lax.axis_index("attn")
    tok_rows, width = tok_ref.shape
    hidden = gate_ref.shape[1]
    slots = experts * cap
    last = attn - 1

    def device(step):
        return (partner_of(me, step, experts), za)

    def block(index):
        return pl.ds(pl.multiple_of(index * cap, cap), cap)

    barrier = pltpu.get_barrier_semaphore()
    for step in range(1, experts):
        pl.semaphore_signal(barrier, inc=1, device_id=device(step), device_id_type=MESH)
    for step in range(1, attn):
        pl.semaphore_signal(
            barrier, inc=1, device_id=(me, lax.rem(za + step, attn)), device_id_type=MESH
        )

    def x_copy(step):
        dst = partner_of(me, step, experts)
        return pltpu.make_async_remote_copy(
            x_send.at[block(dst)], x_all.at[block(step)], x_ss.at[step], x_rs.at[step],
            device_id=(dst, za), device_id_type=MESH,
        )

    def z_copy(step):
        dst = partner_of(me, step, experts)
        return pltpu.make_async_remote_copy(
            z_send.at[block(dst)], z_all.at[block(step)], z_ss.at[step], z_rs.at[step],
            device_id=(dst, za), device_id_type=MESH,
        )

    def right_copy(src, piece):
        return pltpu.make_async_remote_copy(
            src.at[piece], from_left.at[piece], r_ss.at[piece], r_rs.at[piece],
            device_id=(me, lax.rem(za + 1, attn)), device_id_type=MESH,
        )

    def left_copy(src, piece):
        return pltpu.make_async_remote_copy(
            src.at[piece], from_right.at[piece], l_ss.at[piece], l_rs.at[piece],
            device_id=(me, lax.rem(za + attn - 1, attn)), device_id_type=MESH,
        )

    def term_copy(step):
        return pltpu.make_async_remote_copy(
            term_send.at[block(step)], term_back.at[block(me)], t_ss.at[step], t_rs.at[step],
            device_id=device(step), device_id_type=MESH,
        )

    def score_copy(step):
        return pltpu.make_async_remote_copy(
            score_send, score_back.at[za], s_ss.at[step], s_rs.at[step],
            device_id=(me, lax.rem(za + step, attn)), device_id_type=MESH,
        )

    ids = ids_ref[...]
    lanes = lax.broadcasted_iota(jnp.int32, (tok_rows, slots), 1)
    first, second = ids[:, 0:1], ids[:, 1:2]
    named = (lanes[:, :128] == first).astype(F32), (lanes[:, :128] == second).astype(F32)
    rows = lax.broadcasted_iota(jnp.int32, (tok_rows, tok_rows), 0)
    cols = lax.broadcasted_iota(jnp.int32, (tok_rows, tok_rows), 1)
    earlier = (cols < rows).astype(BF16)
    count = jnp.dot(earlier, (named[0] + named[1]).astype(BF16), preferred_element_type=F32)
    for j, expert in enumerate((first, second)):
        rank = jnp.sum(count * named[j], axis=1, keepdims=True).astype(jnp.int32)
        place[j] = (lanes == expert * cap + rank).astype(F32).astype(BF16)
    place_0, place_1 = place[0], place[1]
    weight = wt_ref[...].astype(F32)
    upstream = cot_ref[...].astype(F32)
    x_send[...] = contract_rows(place_0 + place_1, tok_ref[...]).astype(BF16)
    pl.semaphore_wait(barrier, experts - 1 + attn - 1)
    for step in range(1, experts):
        x_copy(step).start()
    z_send[...] = (
        contract_rows(place_0, (weight[:, 0:1] * upstream).astype(BF16))
        + contract_rows(place_1, (weight[:, 1:2] * upstream).astype(BF16))
    ).astype(BF16)
    for step in range(1, experts):
        z_copy(step).start()
    x_all[block(0)] = x_send[block(me)]
    z_all[block(0)] = z_send[block(me)]
    share = hidden // attn
    lane = lax.broadcasted_iota(jnp.int32, (1, hidden), 1)
    mine = jnp.logical_and(lane >= za * share, lane < (za + 1) * share).astype(F32)

    def send_out(piece):
        @pl.when(za == 0)
        def _():
            right_copy(own, piece).start()

        @pl.when(za == last)
        def _():
            left_copy(own, piece).start()

    def pass_right(piece):
        right_copy(own, piece).wait_recv()
        to_right[piece] = (from_left[piece].astype(F32) + own[piece].astype(F32)).astype(BF16)
        right_copy(to_right, piece).start()

    def pass_left(piece):
        left_copy(own, piece).wait_recv()
        to_left[piece] = (from_right[piece].astype(F32) + own[piece].astype(F32)).astype(BF16)
        left_copy(to_left, piece).start()

    middle = jnp.logical_and(za > 0, za < last)
    low = 2 * za < attn

    def forward(chunk):
        @pl.when(chunk > 0)
        def _():
            x_copy(chunk).wait_recv()
            z_copy(chunk).wait_recv()

        feat, scaled = x_all[block(chunk)], z_all[block(chunk)]
        own[3 * chunk] = jnp.dot(feat, gate_ref[...], preferred_element_type=F32).astype(BF16)
        send_out(3 * chunk)
        own[3 * chunk + 1] = jnp.dot(feat, up_ref[...], preferred_element_type=F32).astype(BF16)
        send_out(3 * chunk + 1)
        own[3 * chunk + 2] = contract_columns(scaled, down_ref[...]).astype(BF16)
        send_out(3 * chunk + 2)

    def relay(chunk, near):
        for part in range(3):
            piece = 3 * chunk + part

            @pl.when(jnp.logical_and(middle, low if near else jnp.logical_not(low)))
            def _():
                pass_right(piece)

            @pl.when(jnp.logical_and(middle, jnp.logical_not(low) if near else low))
            def _():
                pass_left(piece)

    def finish(chunk):
        for part in range(3):
            piece = 3 * chunk + part
            sums[part] = own[piece].astype(F32)

            @pl.when(za > 0)
            def _():
                @pl.when(za == last)
                def _():
                    right_copy(own, piece).wait_recv()

                sums[part] = sums[part] + from_left[piece].astype(F32)

            @pl.when(za < last)
            def _():
                @pl.when(za == 0)
                def _():
                    left_copy(own, piece).wait_recv()

                sums[part] = sums[part] + from_right[piece].astype(F32)

        gate, up, back = sums[0], sums[1], sums[2]
        sig = 1.0 / (1.0 + jnp.exp(-gate))
        silu = gate * sig
        act = (silu * up).astype(BF16)
        grad_g = (back * up * sig * (1.0 + gate * (1.0 - sig))).astype(BF16)
        grad_u = (back * silu).astype(BF16)
        act_all[block(chunk)] = act
        gg_all[block(chunk)] = grad_g
        gu_all[block(chunk)] = grad_u
        term = contract_columns(grad_g, gate_ref[...]) + contract_columns(grad_u, up_ref[...])
        score = jnp.sum(act.astype(F32) * back * mine, axis=1, keepdims=True)
        term_send[block(chunk), :width] = term.astype(BF16)
        term_send[block(chunk), width:] = jnp.broadcast_to(score, (cap, 128)).astype(BF16)

        @pl.when(chunk > 0)
        def _():
            term_copy(chunk).start()

        @pl.when(chunk == 0)
        def _():
            term_back[block(me)] = term_send[block(0)]

    half = experts // 2 * cap

    def add_grad(acc, left, right, part):
        lhs = left[pl.ds(part * half, half)]
        step = 256 if right.shape[1] % 256 == 0 else 128
        for at in range(0, right.shape[1], step):
            done = contract_rows(lhs, right[pl.ds(part * half, half), at : at + step])
            if part:
                done = acc[:, at : at + step] + done
            acc[:, at : at + step] = done

    def body(step, carry):
        @pl.when(step < experts)
        def _():
            forward(step)

        @pl.when(jnp.logical_and(step >= 1, step < experts + 1))
        def _():
            relay(step - 1, True)

        @pl.when(jnp.logical_and(step >= 2, step < experts + 2))
        def _():
            relay(step - 2, False)

        @pl.when(step >= LAG)
        def _():
            finish(step - LAG)

        @pl.when(step == LAG + experts // 2 - 1)
        def _():
            add_grad(acc_gate, x_all, gg_all, 0)
            add_grad(acc_up, x_all, gu_all, 0)
            add_grad(acc_down, act_all, z_all, 0)

        return carry

    lax.fori_loop(0, experts + LAG, body, 0)

    add_grad(acc_gate, x_all, gg_all, 1)
    gate_out = pltpu.make_async_copy(acc_gate, ggate_ref, out_sem.at[0])
    gate_out.start()
    add_grad(acc_up, x_all, gu_all, 1)
    up_out = pltpu.make_async_copy(acc_up, gup_ref, out_sem.at[1])
    up_out.start()

    for step in range(1, experts):
        term_copy(step).wait_recv()
    place_0, place_1 = place[0], place[1]
    scores = term_back[:, width:]
    score_0 = jnp.dot(place_0, scores, preferred_element_type=F32)
    score_1 = jnp.dot(place_1, scores, preferred_element_type=F32)
    lane = lax.broadcasted_iota(jnp.int32, (tok_rows, 128), 1)
    score_send[...] = jnp.transpose(jnp.where(lane == 0, score_0, score_1))[:8]
    for step in range(1, attn):
        score_copy(step).start()
    score_back[za] = score_send[...]
    gtok_ref[...] = jnp.dot(
        place_0 + place_1, term_back[:, :width], preferred_element_type=F32
    ).astype(BF16)
    add_grad(acc_down, act_all, z_all, 1)
    down_out = pltpu.make_async_copy(acc_down, gdown_ref, out_sem.at[2])
    down_out.start()
    for step in range(1, attn):
        score_copy(step).wait_recv()
    total = score_back[0]
    for index in range(1, attn):
        total = total + score_back[index]
    route_ref[...] = jnp.transpose(total)[:, :2] / wt_ref[...].astype(F32)

    for step in range(1, experts):
        x_copy(step).wait_send()
        z_copy(step).wait_send()
        term_copy(step).wait_send()
    for step in range(1, attn):
        score_copy(step).wait_send()

    def drain(piece, carry):
        @pl.when(za < last)
        def _():
            right_copy(own, piece).wait_send()

        @pl.when(za > 0)
        def _():
            left_copy(own, piece).wait_send()

        return carry

    lax.fori_loop(0, 3 * experts, drain, 0)
    gate_out.wait()
    up_out.wait()
    down_out.wait()


def fused_shards(experts, attn, tokens, cotangent, expert_ids, route_weight, gate_weight, up_weight, down_weight):
    tok_rows, width = tokens.shape
    per_token = expert_ids.shape[1]
    cap = 3 * tok_rows * per_token // (2 * experts)
    hidden = gate_weight.shape[2]
    slots = experts * cap
    dma = pltpu.SemaphoreType.DMA
    vmem = pl.BlockSpec(memory_space=pltpu.VMEM)
    anywhere = pl.BlockSpec(memory_space=pl.ANY)
    pieces = pltpu.VMEM((3 * experts, cap, hidden), BF16)
    grads = pl.pallas_call(
        functools.partial(block_kernel, experts, attn, cap),
        out_shape=(
            jax.ShapeDtypeStruct((tok_rows, width), BF16),
            jax.ShapeDtypeStruct((tok_rows, per_token), F32),
            jax.ShapeDtypeStruct((width, hidden), F32),
            jax.ShapeDtypeStruct((width, hidden), F32),
            jax.ShapeDtypeStruct((hidden, width), F32),
        ),
        in_specs=[vmem] * 7,
        out_specs=(vmem, vmem, anywhere, anywhere, anywhere),
        scratch_shapes=[
            pltpu.VMEM((slots, width), BF16),
            pltpu.VMEM((slots, width), BF16),
            pltpu.VMEM((slots, width), BF16),
            pltpu.VMEM((slots, width), BF16),
            pieces, pieces, pieces, pieces, pieces,
            pltpu.VMEM((3, cap, hidden), F32),
            pltpu.VMEM((slots, hidden), BF16),
            pltpu.VMEM((slots, hidden), BF16),
            pltpu.VMEM((slots, hidden), BF16),
            pltpu.VMEM((slots, width + 128), BF16),
            pltpu.VMEM((slots, width + 128), BF16),
            pltpu.VMEM((width, hidden), F32),
            pltpu.VMEM((width, hidden), F32),
            pltpu.VMEM((hidden, width), F32),
            pltpu.VMEM((per_token, tok_rows, slots), BF16),
            pltpu.VMEM((8, tok_rows), F32),
            pltpu.VMEM((attn, 8, tok_rows), F32),
            dma((experts,)), dma((experts,)), dma((experts,)), dma((experts,)),
            dma((3 * experts,)), dma((3 * experts,)), dma((3 * experts,)), dma((3 * experts,)),
            dma((experts,)), dma((experts,)),
            dma((attn,)), dma((attn,)), dma((3,)),
        ],
        compiler_params=pltpu.CompilerParams(
            collective_id=0, has_side_effects=True, vmem_limit_bytes=48 * 1024 * 1024
        ),
        cost_estimate=pl.CostEstimate(
            flops=16 * slots * width * hidden, bytes_accessed=18 * width * hidden, transcendentals=slots * hidden
        ),
    )(tokens, cotangent, expert_ids, route_weight, gate_weight[0], up_weight[0], down_weight[0])
    return (grads[0], grads[1], grads[2][None], grads[3][None], grads[4][None])


def swiglu_grads(summed, hidden):
    gate_part = summed[:, :hidden]
    up_part = summed[:, hidden : 2 * hidden]
    back_part = summed[:, 2 * hidden :]
    sigmoid_gate = jax.nn.sigmoid(gate_part)
    silu_gate = gate_part * sigmoid_gate
    activation = silu_gate * up_part
    grad_g = back_part * up_part * sigmoid_gate * (1.0 + gate_part * (1.0 - sigmoid_gate))
    grad_u = back_part * silu_gate
    return jnp.concatenate([activation, grad_g, grad_u], axis=1).astype(jnp.bfloat16)


def shards(tokens, cotangent, expert_ids, route_weight, gate_weight, up_weight, down_weight):
    tok_rows, width_share = tokens.shape
    per_token = expert_ids.shape[1]
    experts = lax.axis_size("exp")
    capacity = 3 * tok_rows * per_token // (2 * experts)
    hidden = gate_weight.shape[2]
    slot_total = experts * capacity
    routed = expert_ids.reshape(-1)
    one_hot = (routed[:, None] == jnp.arange(experts, dtype=jnp.int32)[None, :]).astype(jnp.int32)
    ranked = jnp.cumsum(one_hot, axis=0) - 1
    slot_pos = jnp.sum(ranked * one_hot, axis=1)
    target = routed * capacity + slot_pos
    feat_send = (
        jnp.zeros((slot_total, width_share), jnp.bfloat16)
        .at[target]
        .set(jnp.repeat(tokens, per_token, axis=0))
    )
    upstream_send = (
        jnp.zeros((slot_total, width_share), jnp.bfloat16)
        .at[target]
        .set(jnp.repeat(cotangent, per_token, axis=0))
    )
    weight_send = jnp.zeros((slot_total,), jnp.bfloat16).at[target].set(route_weight.reshape(-1))
    feat_recv, upstream_recv, weight_recv = (
        lax.all_to_all(
            feat_send.reshape(experts, capacity, width_share),
            "exp",
            split_axis=0,
            concat_axis=0,
            tiled=True,
        ),
        lax.all_to_all(
            upstream_send.reshape(experts, capacity, width_share),
            "exp",
            split_axis=0,
            concat_axis=0,
            tiled=True,
        ),
        lax.all_to_all(
            weight_send.reshape(experts, capacity), "exp", split_axis=0, concat_axis=0, tiled=True
        ),
    )
    feat_rows = feat_recv.reshape(slot_total, width_share)
    upstream_rows = upstream_recv.reshape(slot_total, width_share)
    weight_rows = weight_recv.reshape(slot_total)
    scaled_rows = (
        weight_rows[:, None].astype(jnp.float32) * upstream_rows.astype(jnp.float32)
    ).astype(jnp.bfloat16)
    joint_weight = jnp.concatenate([gate_weight[0], up_weight[0]], axis=1)
    down_share = down_weight[0]
    feat_block = feat_rows
    scaled_block = scaled_rows
    gate_up = jnp.dot(feat_block, joint_weight, preferred_element_type=jnp.float32)
    back_hidden = lax.dot_general(
        scaled_block, down_share, (((1,), (1,)), ((), ())), preferred_element_type=jnp.float32
    )
    summed = lax.psum(
        jnp.concatenate([gate_up, back_hidden], axis=1).astype(jnp.bfloat16), "attn"
    ).astype(jnp.float32)
    act_rows = swiglu_grads(summed, hidden)
    feat_block = feat_rows
    scaled_block = scaled_rows
    activation = act_rows[:, :hidden]
    grad_pair = act_rows[:, hidden:]
    grad_joint = lax.dot_general(
        feat_block, grad_pair, (((0,), (0,)), ((), ())), preferred_element_type=jnp.float32
    )
    grad_down_part = lax.dot_general(
        activation, scaled_block, (((0,), (0,)), ((), ())), preferred_element_type=jnp.float32
    )
    token_block = lax.dot_general(
        grad_pair, joint_weight, (((1,), (1,)), ((), ())), preferred_element_type=jnp.float32
    ).astype(jnp.bfloat16)
    out_block = jnp.dot(activation, down_share, preferred_element_type=jnp.float32)
    score_block = jnp.sum(upstream_rows.astype(jnp.float32) * out_block, axis=1).astype(
        jnp.bfloat16
    )
    totals = (grad_joint, grad_down_part, token_block, score_block)
    grad_joint, grad_down_share, token_rows, score_rows = totals
    token_back, score_back = (
        lax.all_to_all(
            token_rows.reshape(experts, capacity, width_share),
            "exp",
            split_axis=0,
            concat_axis=0,
            tiled=True,
        ),
        lax.all_to_all(
            score_rows.reshape(experts, capacity), "exp", split_axis=0, concat_axis=0, tiled=True
        ),
    )
    token_choice = token_back.reshape(slot_total, width_share)[target]
    grad_tokens = jnp.sum(
        token_choice.reshape(tok_rows, per_token, width_share).astype(jnp.float32), axis=1
    ).astype(jnp.bfloat16)
    score_choice = score_back.reshape(slot_total)[target].reshape(tok_rows, per_token)
    grad_route = lax.psum(score_choice.astype(jnp.float32), "attn")
    grad_gate = grad_joint[:, :hidden][None]
    grad_up = grad_joint[:, hidden:][None]
    return (grad_tokens, grad_route, grad_gate, grad_up, grad_down_share[None])


def fits(experts, attn, tokens, expert_ids, hidden):
    rows, width = tokens.shape[0] // experts, tokens.shape[1] // attn
    cap = 3 * rows * expert_ids.shape[1] // (2 * experts)
    return (
        experts & (experts - 1) == 0
        and 2 <= experts <= 128
        and attn >= 2
        and expert_ids.shape[1] == 2
        and rows == 128
        and cap % 16 == 0
        and width % 128 == 0
        and hidden % (128 * attn) % 128 == 0
        and hidden % attn == 0
    )


def solution(mesh):
    experts, attn = mesh.shape["exp"], mesh.shape["attn"]

    in_specs = (
        P("exp", "attn"),
        P("exp", "attn"),
        P("exp", None),
        P("exp", None),
        P("exp", "attn", None),
        P("exp", "attn", None),
        P("exp", None, "attn"),
    )
    out_specs = (
        P("exp", "attn"),
        P("exp", None),
        P("exp", "attn", None),
        P("exp", "attn", None),
        P("exp", None, "attn"),
    )

    def whole(tokens, cotangent, expert_ids, route_weight, gate_weight, up_weight, down_weight):
        args = (tokens, cotangent, expert_ids, route_weight, gate_weight, up_weight, down_weight)
        part = shards
        if fits(experts, attn, tokens, expert_ids, gate_weight.shape[2]):
            part = functools.partial(fused_shards, experts, attn)
        return jax.shard_map(
            part, mesh=mesh, in_specs=in_specs, out_specs=out_specs, check_vma=False
        )(*args)

    return whole
```
